768 devices in a mesh: dp: 2 (over core), seq: 4 (over x), tensor: 96 (over y, z).
Axes of the slice: x: 4, y: 8, z: 12, core: 2. Of those that a mesh axis runs over, the one named last changes fastest.
Arguments:
- inputs: bfloat16 [1024, 12288], P(('dp', 'seq')), may hold values from -6 to 6
- out_grad: bfloat16 [1024, 12288], P(('dp', 'seq')), may hold values from -6 to 6
- up_blocks: bfloat16 [192, 24, 128, 128], P('tensor'), may hold values from -0.109375 to 0.109375
- down_blocks: bfloat16 [192, 24, 128, 128], P('tensor'), may hold values from -0.09375 to 0.09375
- up_rows: int32 [192, 24], P('tensor'), may hold values from 0 to 95, as said below
- down_cols: int32 [192, 24], P('tensor'), may hold values from 0 to 95, as said below
- slot_count: int32 [96], P('tensor'), may hold values from 1 to 2, as said below
Outputs:
- input_grad: bfloat16 [1024, 12288], P(('dp', 'seq'), 'tensor')
- up_grad: bfloat16 [192, 24, 128, 128], P('tensor', ('dp', 'seq'))
- down_grad: bfloat16 [192, 24, 128, 128], P('tensor', ('dp', 'seq'))
The draws below stay inside these ranges and needn't reach their ends.
Inputs may be any that keep to these rules, and one draw needn't show every extreme that they name: `up_rows`: each row names 24 different block numbers. `down_cols`: each row names 24 different block numbers. `slot_count`: half of the owners hold 1 and half hold 2; the counts sum to 144. Slots at or beyond an owner's count hold no hidden block.
All inputs are finite; a program needn't handle non-finite values.
Results may differ from the reference program's by a relative error of at most 0.017.
Values may be sent and summed in bfloat16 or wider, within the bound.
No kernel may reach another device: no remote copies, remote signals or barrier semaphores. Data moves between devices by JAX's collectives and lax.ppermute only.
A program may use at most 64 MiB of HBM per device.

```python
import jax
import jax.numpy as jnp
from jax import lax

D = 12288
BLK = 128
FAN = 24
SLOTS = 2
FF = 18432
TOK_DEV = 128
TOKENS = 1024
N_DP = 2
N_SEQ = 4
N_TENSOR = 96


def block_lists(key, count_rows):
    key_list = jax.random.split(key, count_rows)
    return jax.vmap(lambda one_key: jax.random.permutation(one_key, D // BLK)[:FAN])(key_list).astype(jnp.int32)


def draw_up_rows(key, part):
    key = jax.random.fold_in(key, 11)
    return block_lists(key, N_TENSOR * SLOTS)


def draw_down_cols(key, part):
    key = jax.random.fold_in(key, 23)
    return block_lists(key, N_TENSOR * SLOTS)


def draw_slot_count(key, part):
    key = jax.random.fold_in(key, 37)
    placing = jax.random.permutation(key, N_TENSOR)
    values = 1 + (jnp.arange(N_TENSOR, dtype=jnp.int32) < N_TENSOR // 2).astype(jnp.int32)
    return jnp.zeros((N_TENSOR,), jnp.int32).at[placing].set(values)


def block_scale(key, shape, cuts, low, high):
    def one(dim, shards_of):
        heights = jax.random.uniform(jax.random.fold_in(jax.random.fold_in(key, 6), dim), (shards_of,), jnp.float32, low / len(cuts), high / len(cuts))
        return jnp.repeat(jnp.exp(heights), shape[dim] // shards_of).reshape((-1,) + (1,) * (len(shape) - dim - 1))

    gain = one(*cuts[0])
    for cut in cuts[1:]:
        gain = gain * one(*cut)
    return gain


def noise(own_key, extent, width, limit, pieces=(), kind=jnp.bfloat16):
    entries = jax.random.normal(own_key, extent, jnp.float32) * width
    if len(pieces) > 0:
        entries = block_scale(own_key, extent, pieces, -0.22, 0.18) * entries
    return jnp.clip(entries, min=-limit, max=limit).astype(kind)


def setup_inputs(seed: int = 0) -> dict:
    seeds = jax.random.split(jax.random.key(seed), 8)
    inputs = noise(seeds[0], (TOKENS, D), 1.0, 6.0, ((0, 8),))
    out_grad = noise(seeds[1], (TOKENS, D), 1.0, 6.0, ((0, 8),))
    up_blocks = noise(seeds[2], (N_TENSOR * SLOTS, FAN, BLK, BLK), (FAN * BLK) ** -0.5, 0.109375, ((0, 96),))
    down_blocks = noise(seeds[3], (N_TENSOR * SLOTS, FAN, BLK, BLK), (FF // 4) ** -0.5, 0.09375, ((0, 96),))
    up_rows = draw_up_rows(jax.random.fold_in(seeds[7], 71), 0)
    down_cols = draw_down_cols(jax.random.fold_in(seeds[7], 71), 0)
    slot_count = draw_slot_count(jax.random.fold_in(seeds[7], 71), 0)
    return {"inputs": inputs, "out_grad": out_grad, "up_blocks": up_blocks, "down_blocks": down_blocks, "up_rows": up_rows, "down_cols": down_cols, "slot_count": slot_count}


def gelu_value(pre_act):
    argument = 0.7978845608 * (pre_act + 0.044715 * pre_act * pre_act * pre_act)
    return 0.5 * pre_act * (1.0 + jnp.tanh(argument))


def gelu_slope(pre_act):
    argument = 0.7978845608 * (pre_act + 0.044715 * pre_act * pre_act * pre_act)
    tangent = jnp.tanh(argument)
    return 0.5 * (1.0 + tangent) + 0.5 * pre_act * (1.0 - tangent * tangent) * 0.7978845608 * (1.0 + 3.0 * 0.044715 * pre_act * pre_act)


def group_sum(terms):
    rounded = lax.optimization_barrier(terms.astype(jnp.bfloat16))
    return jnp.sum(rounded.astype(jnp.float32), axis=0).astype(jnp.bfloat16)


def reference(inputs, out_grad, up_blocks, down_blocks, up_rows, down_cols, slot_count):
    highest = lax.Precision.HIGHEST
    group_count = N_DP * N_SEQ
    block_count = D // BLK
    input_blocks = inputs.reshape(TOKENS, block_count, BLK)
    grad_blocks = out_grad.reshape(TOKENS, block_count, BLK)
    owner_up = up_blocks.reshape(N_TENSOR, SLOTS, FAN, BLK, BLK)
    owner_down = down_blocks.reshape(N_TENSOR, SLOTS, FAN, BLK, BLK)
    owner_rows = up_rows.reshape(N_TENSOR, SLOTS, FAN)
    owner_cols = down_cols.reshape(N_TENSOR, SLOTS, FAN)

    def one_owner(running, packed):
        ups, downs, rows_here, cols_here, count_now = packed
        live_mask = (jnp.arange(SLOTS, dtype=jnp.int32) < count_now).astype(jnp.float32)[:, None, None]
        input_taken = input_blocks[:, rows_here, :].astype(jnp.float32)
        grad_taken = grad_blocks[:, cols_here, :].astype(jnp.float32)
        pre_act = jnp.einsum("tskc,skcb->stb", input_taken, ups.astype(jnp.float32), precision=highest)
        hidden = (gelu_value(pre_act) * live_mask).astype(jnp.bfloat16)
        hid_grad = jnp.einsum("tskj,skbj->stb", grad_taken, downs.astype(jnp.float32), precision=highest)
        pre_grad = (hid_grad * gelu_slope(pre_act) * live_mask).astype(jnp.bfloat16)
        hidden_groups = hidden.astype(jnp.float32).reshape(SLOTS, group_count, TOK_DEV, BLK)
        pre_groups = pre_grad.astype(jnp.float32).reshape(SLOTS, group_count, TOK_DEV, BLK)
        grad_groups = grad_taken.reshape(group_count, TOK_DEV, SLOTS, FAN, BLK)
        input_groups = input_taken.reshape(group_count, TOK_DEV, SLOTS, FAN, BLK)
        down_terms = jnp.einsum("sgtb,gtskj->gskbj", hidden_groups, grad_groups, precision=highest)
        up_terms = jnp.einsum("gtskc,sgtb->gskcb", input_groups, pre_groups, precision=highest)
        products = jnp.einsum("stb,skcb->sktc", pre_grad.astype(jnp.float32), ups.astype(jnp.float32), precision=highest)
        flat = products.reshape(SLOTS * FAN, TOKENS, BLK)
        placed = jax.ops.segment_sum(flat, rows_here.reshape(SLOTS * FAN), num_segments=block_count)
        running = running + jnp.transpose(placed, (1, 0, 2)).reshape(TOKENS, D)
        return running, (group_sum(up_terms), group_sum(down_terms))

    start = jnp.zeros((TOKENS, D), jnp.float32)
    summed, grads = lax.scan(one_owner, start, (owner_up, owner_down, owner_rows, owner_cols, slot_count))
    up_grad = grads[0].reshape(N_TENSOR * SLOTS, FAN, BLK, BLK)
    down_grad = grads[1].reshape(N_TENSOR * SLOTS, FAN, BLK, BLK)
    return summed.astype(jnp.bfloat16), up_grad, down_grad
```

```python
import jax
import jax.numpy as jnp
from jax import lax
from jax.experimental import pallas as pl
from jax.experimental.pallas import tpu as pltpu
from jax.sharding import Mesh
from jax.sharding import PartitionSpec as P

BLK = 128
N_DP, N_SEQ, N_Y, N_Z = 2, 4, 8, 12
TOKENS_AX = ("dp", "seq")
OWNER_AX = ("ya", "yb", "yc", "za", "zb", "zc")
VMEM_LIMIT = 48 * 1024 * 1024


def gelu_pair(pre_act):
    squared = pre_act * pre_act
    tangent = jnp.tanh(0.7978845608 * (pre_act + 0.044715 * squared * pre_act))
    value = 0.5 * pre_act * (1.0 + tangent)
    slope = 0.5 * (1.0 + tangent) + 0.5 * pre_act * (1.0 - tangent * tangent) * 0.7978845608 * (
        1.0 + 3.0 * 0.044715 * squared
    )
    return value, slope


def two_blocks(ref, first, second):
    return jnp.concatenate(
        [
            ref[:, pl.ds(pl.multiple_of(first * BLK, BLK), BLK)],
            ref[:, pl.ds(pl.multiple_of(second * BLK, BLK), BLK)],
        ],
        axis=1,
    )


def dot_nn(left, right):
    return lax.dot_general(left, right, (((1,), (0,)), ((), ())), preferred_element_type=jnp.float32)


def dot_nt(left, right):
    return lax.dot_general(left, right, (((1,), (1,)), ((), ())), preferred_element_type=jnp.float32)


def place_of(r, core):
    y, z = r // N_Z, r % N_Z
    near = ((y % 2) ^ core) * 2 + ((z % 2) ^ core)
    mid = (((y // 2) % 2) ^ core) * 2 + (((z // 2) % 2) ^ core)
    return (near * 4 + mid) * 6 + (y // 4) * 3 + z // 4


def layer_kernel(core, rows, cols, count, inputs, out_grad, ups, downs, placed, parts):
    slots, fan = rows.shape
    tok = inputs.shape[0]
    each = parts.shape[3]
    placed[...] = jnp.zeros_like(placed)
    for s in range(slots):
        live = (s < count[0]).astype(jnp.float32)
        pre_act = jnp.zeros((tok, BLK), jnp.float32)
        hid_grad = jnp.zeros((tok, BLK), jnp.float32)
        for k in range(0, fan, 2):
            pre_act += dot_nn(two_blocks(inputs, rows[s, k], rows[s, k + 1]), ups[s, k * BLK : (k + 2) * BLK, :])
            hid_grad += dot_nt(
                two_blocks(out_grad, cols[s, k], cols[s, k + 1]),
                jnp.concatenate([downs[s, k * BLK : (k + 1) * BLK, :], downs[s, (k + 1) * BLK : (k + 2) * BLK, :]], axis=1),
            )
        value, slope = gelu_pair(pre_act)
        pre_grad = hid_grad * slope * live
        hidden_t = jnp.transpose(value * live).astype(jnp.bfloat16)
        pre_grad_t = jnp.transpose(pre_grad).astype(jnp.bfloat16)
        pre_grad = pre_grad.astype(jnp.bfloat16)
        for k in range(0, fan, 2):
            both = dot_nt(pre_grad, ups[s, k * BLK : (k + 2) * BLK, :])
            for i in range(2):
                at = place_of(rows[s, k + i], core[0])
                product = both[:, i * BLK : (i + 1) * BLK]
                if s > 0:
                    product += placed[at].astype(jnp.float32)
                placed[at] = product.astype(jnp.bfloat16)
        for k in range(0, fan, 2):
            up = dot_nn(pre_grad_t, two_blocks(inputs, rows[s, k], rows[s, k + 1]))
            down = dot_nn(hidden_t, two_blocks(out_grad, cols[s, k], cols[s, k + 1]))
            for i in range(2):
                piece = slice(i * BLK, (i + 1) * BLK)
                parts[(k + i) // each, 0, s, (k + i) % each] = up[:, piece].astype(jnp.bfloat16)
                parts[(k + i) // each, 1, s, (k + i) % each] = down[:, piece].astype(jnp.bfloat16)


def owner_groups(step_y, count_y, step_z, count_z):
    groups = []
    for core in range(N_DP):
        for seq in range(N_SEQ):
            for y in range(N_Y):
                for z in range(N_Z):
                    if (y // step_y) % count_y or (z // step_z) % count_z:
                        continue
                    groups.append(
                        [
                            ((core * N_SEQ + seq) * N_Y + (y + (i + core) * step_y) % N_Y) * N_Z
                            + (z + (j + core) * step_z) % N_Z
                            for i in range(count_y)
                            for j in range(count_z)
                        ]
                    )
    return groups


def sum_first(terms):
    total = terms[0].astype(jnp.float32)
    for i in range(1, terms.shape[0]):
        total += terms[i].astype(jnp.float32)
    return total.astype(jnp.bfloat16)


def local(inputs, out_grad, up_blocks, down_blocks, up_rows, down_cols, slot_count):
    tok, features = inputs.shape
    slots, fan = up_rows.shape
    groups = N_DP * N_SEQ
    each = fan // groups
    smem = pl.BlockSpec(memory_space=pltpu.SMEM)
    vmem = pl.BlockSpec(memory_space=pltpu.VMEM)
    core = lax.axis_index("dp").astype(jnp.int32).reshape(1)
    placed, parts = pl.pallas_call(
        layer_kernel,
        out_shape=(
            jax.ShapeDtypeStruct((N_Y * N_Z, tok, BLK), jnp.bfloat16),
            jax.ShapeDtypeStruct((groups, 2, slots, each, BLK, BLK), jnp.bfloat16),
        ),
        in_specs=[smem] * 4 + [vmem] * 4,
        out_specs=(vmem,) * 2,
        compiler_params=pltpu.CompilerParams(vmem_limit_bytes=VMEM_LIMIT),
    )(
        core,
        up_rows,
        down_cols,
        slot_count,
        inputs,
        out_grad,
        up_blocks.reshape(slots, fan * BLK, BLK),
        down_blocks.reshape(slots, fan * BLK, BLK),
    )
    summed = lax.psum_scatter(parts, TOKENS_AX, scatter_dimension=0)
    up_grad = jnp.swapaxes(summed[0], 2, 3)
    down_grad = summed[1]

    everyone = TOKENS_AX + OWNER_AX
    near = lax.all_to_all(
        placed.reshape(4, 24, tok, BLK), everyone, 0, 0, axis_index_groups=owner_groups(1, 2, 1, 2)
    )
    near = sum_first(near)
    mid = lax.all_to_all(near.reshape(4, 6, tok, BLK), everyone, 0, 0, axis_index_groups=owner_groups(2, 2, 2, 2))
    mid = sum_first(mid)
    far = lax.all_to_all(mid, ("ya", "za"), 0, 0)
    input_grad = sum_first(far)
    return input_grad, up_grad, down_grad


def solution(mesh):
    split = Mesh(mesh.devices.reshape(N_DP, N_SEQ, 2, 2, 2, 3, 2, 2), TOKENS_AX + OWNER_AX)
    in_specs = (
        P(TOKENS_AX, None),
        P(TOKENS_AX, None),
        P(OWNER_AX, None, None, None),
        P(OWNER_AX, None, None, None),
        P(OWNER_AX, None),
        P(OWNER_AX, None),
        P(OWNER_AX),
    )
    out_specs = (
        P(TOKENS_AX, OWNER_AX),
        P(OWNER_AX, TOKENS_AX, None, None),
        P(OWNER_AX, TOKENS_AX, None, None),
    )
    return jax.shard_map(local, mesh=split, in_specs=in_specs, out_specs=out_specs, check_vma=False)
```

```python
import jax
import jax.numpy as jnp
from jax import lax
from jax.experimental import pallas as pl
from jax.experimental.pallas import tpu as pltpu
from jax.sharding import Mesh
from jax.sharding import PartitionSpec as P

BLK = 128
VMEM_LIMIT = 60 * 1024 * 1024
N_DP, N_SEQ, N_Y, N_Z = 2, 4, 8, 12
TOKENS_AX = ("dp", "seq")
OWNER_AX = ("y", "z")


def gelu_pair(pre_act):
    squared = pre_act * pre_act
    tangent = jnp.tanh(0.7978845608 * (pre_act + 0.044715 * squared * pre_act))
    value = 0.5 * pre_act * (1.0 + tangent)
    slope = 0.5 * (1.0 + tangent) + 0.5 * pre_act * (1.0 - tangent * tangent) * 0.7978845608 * (
        1.0 + 3.0 * 0.044715 * squared
    )
    return value, slope


def two_blocks(ref, first, second):
    return jnp.concatenate(
        [
            ref[:, pl.ds(pl.multiple_of(first * BLK, BLK), BLK)],
            ref[:, pl.ds(pl.multiple_of(second * BLK, BLK), BLK)],
        ],
        axis=1,
    )


def fetch_columns(source, indices, target, sem):
    for i, index in enumerate(indices):
        columns = source.at[:, pl.ds(pl.multiple_of(index * BLK, BLK), BLK)]
        pltpu.make_async_copy(columns, target.at[i], sem).start()


def wait_for(target, sem):
    pltpu.make_async_copy(target, target, sem).wait()


def dot_nn(left, right):
    return lax.dot_general(left, right, (((1,), (0,)), ((), ())), preferred_element_type=jnp.float32)


def dot_nt(left, right):
    return lax.dot_general(left, right, (((1,), (1,)), ((), ())), preferred_element_type=jnp.float32)


def ring_place(size, far_groups):
    first = [0 if p % 4 in (0, 3) else 1 for p in range(size)]
    third = {p: group.index(p) for group in far_groups for p in group}
    second = {}
    for group in far_groups:
        for p in group:
            second[p] = 0 if min(group) in (0, 1) else 1
    return [(first[p], second[p], third[p]) for p in range(size)]


FAR_Y = [[0, 3], [1, 6], [2, 5], [4, 7]]
FAR_Z = [[p, p + 4, p + 8] for p in range(4)]
PLACE_Y, PLACE_Z = ring_place(N_Y, FAR_Y), ring_place(N_Z, FAR_Z)


def place_table():
    table = []
    for core in range(N_DP):
        for r in range(N_Y * N_Z):
            a, b = PLACE_Y[(r // N_Z - core) % N_Y], PLACE_Z[(r % N_Z - core) % N_Z]
            table.append(((a[0] * 2 + b[0]) * 4 + a[1] * 2 + b[1]) * 6 + a[2] * 3 + b[2])
    return table


def owner_groups(groups_y, groups_z):
    return [
        [
            ((core * N_SEQ + seq) * N_Y + (y + core) % N_Y) * N_Z + (z + core) % N_Z
            for y in group_y
            for z in group_z
        ]
        for core in range(N_DP)
        for seq in range(N_SEQ)
        for group_y in groups_y
        for group_z in groups_z
    ]


def neighbours(size, start, step):
    place = PLACE_Y if size == N_Y else PLACE_Z
    return [sorted((p, (p + 1) % size), key=lambda q: place[q][step]) for p in range(start, size, 2)]


def forward_kernel(
    core, place_hbm, rows_hbm, cols_hbm, count_hbm, inputs_hbm, out_grad_hbm, ups_hbm, downs_hbm,
    placed_hbm, hidden_t, pre_grad_t,
    placed, inputs, out_grad, ups, downs, place, rows, cols, count, small_sems, sems, out_sem,
):
    slots, fan = rows.shape
    tok = inputs.shape[0]
    small = [
        pltpu.make_async_copy(source, target, small_sems.at[i])
        for i, (source, target) in enumerate(
            ((rows_hbm, rows), (cols_hbm, cols), (place_hbm, place), (count_hbm, count))
        )
    ]
    large = [
        pltpu.make_async_copy(source, target, sems.at[i])
        for i, (source, target) in enumerate(
            (
                (ups_hbm.at[0], ups.at[0]),
                (inputs_hbm, inputs),
                (downs_hbm.at[0], downs.at[0]),
                (out_grad_hbm, out_grad),
                (ups_hbm.at[1], ups.at[1]),
                (downs_hbm.at[1], downs.at[1]),
            )
        )
    ]
    for copy in small + large:
        copy.start()
    placed[...] = jnp.zeros_like(placed)
    for copy in small:
        copy.wait()
    for s in range(slots):
        live = (s < count[0]).astype(jnp.float32)
        for copy in large[:2] if s == 0 else large[4:5]:
            copy.wait()
        pre_act = jnp.zeros((tok, BLK), jnp.float32)
        for k in range(0, fan, 2):
            pre_act += dot_nn(
                two_blocks(inputs, rows[s, k], rows[s, k + 1]), ups[s, k * BLK : (k + 2) * BLK, :]
            )
        for copy in large[2:4] if s == 0 else large[5:]:
            copy.wait()
        hid_grad = jnp.zeros((tok, BLK), jnp.float32)
        for k in range(0, fan, 2):
            hid_grad += dot_nt(
                two_blocks(out_grad, cols[s, k], cols[s, k + 1]),
                jnp.concatenate([downs[s, k * BLK : (k + 1) * BLK, :], downs[s, (k + 1) * BLK : (k + 2) * BLK, :]], axis=1),
            )
        value, slope = gelu_pair(pre_act)
        hidden_t[s] = jnp.transpose(value * live).astype(jnp.bfloat16)
        turned = jnp.transpose(hid_grad * slope * live).astype(jnp.bfloat16)
        pre_grad_t[s] = turned
        for k in range(0, fan, 2):
            both = dot_nn(ups[s, k * BLK : (k + 2) * BLK, :], turned)
            for i in range(2):
                at = place[core[0], rows[s, k + i]]
                product = both[i * BLK : (i + 1) * BLK, :]
                if s > 0:
                    product += placed[at].astype(jnp.float32)
                placed[at] = product.astype(jnp.bfloat16)
    write = pltpu.make_async_copy(placed, placed_hbm, out_sem)
    write.start()
    write.wait()


def weight_kernel(
    core, seq, rows, cols, inputs, out_grad,
    hidden_t, pre_grad_t, theirs_far, theirs_near, mine_far, mine_near, fetched, sems,
):
    slots = rows.shape[0]
    parts, each = mine_far.shape[0], mine_far.shape[3]
    here, there = core[0] * N_SEQ, (1 - core[0]) * N_SEQ
    flip, mirror, across = seq[0] ^ 1, 3 - seq[0], seq[0] ^ 2
    first = jnp.where(core[0] == 0, flip, mirror)
    second = flip + mirror - first
    targets = (
        (theirs_far, (there + second, there + across)),
        (theirs_near, (there + seq[0], there + first)),
        (mine_far, (here + first, here + across)),
        (mine_near, (here + seq[0], here + second)),
    )
    for half, (data, ids) in enumerate(((inputs, rows), (out_grad, cols))):
        for t, (_, groups) in enumerate(targets):
            for s in range(slots):
                ks = [group * each + i for group in groups for i in range(each)]
                fetch_columns(data, [ids[s, k] for k in ks], fetched.at[half, t, s], sems.at[half, t])
    for half, left in enumerate((pre_grad_t, hidden_t)):
        for t, (target, _) in enumerate(targets):
            wait_for(fetched.at[half, t], sems.at[half, t])
            for s in range(slots):
                for j in range(0, parts * each, 2):
                    pair = jnp.concatenate([fetched[half, t, s, j], fetched[half, t, s, j + 1]], axis=1)
                    both = dot_nn(left[s], pair)
                    for i in range(2):
                        value = both[:, i * BLK : (i + 1) * BLK]
                        target[(j + i) // each, half, s, (j + i) % each] = value.astype(jnp.bfloat16)


def small_call(kernel, out_shape, *operands):
    vmem = pl.BlockSpec(memory_space=pltpu.VMEM)
    return pl.pallas_call(
        kernel,
        out_shape=out_shape,
        in_specs=[vmem] * len(operands),
        out_specs=jax.tree.map(lambda _: vmem, out_shape),
        compiler_params=pltpu.CompilerParams(vmem_limit_bytes=8 * 1024 * 1024),
    )(*operands)


def sum_first_kernel(terms, total):
    value = terms[0].astype(jnp.float32)
    for i in range(1, terms.shape[0]):
        value += terms[i].astype(jnp.float32)
    total[...] = value.astype(jnp.bfloat16)


def sum_first(terms):
    return small_call(sum_first_kernel, jax.ShapeDtypeStruct(terms.shape[1:], terms.dtype), terms)


def sum_large_kernel(terms_hbm, total, terms, sems):
    steps = sems.shape[0]
    rows = total.shape[0] // steps
    pieces = [pl.ds(i * rows, rows) for i in range(steps)]
    copies = [
        pltpu.make_async_copy(terms_hbm.at[:, piece], terms.at[:, piece], sems.at[i])
        for i, piece in enumerate(pieces)
    ]
    for copy in copies:
        copy.start()
    for copy, piece in zip(copies, pieces):
        copy.wait()
        value = terms[0, piece].astype(jnp.float32)
        for i in range(1, terms.shape[0]):
            value += terms[i, piece].astype(jnp.float32)
        total[piece] = value.astype(jnp.bfloat16)


def sum_large(terms):
    return pl.pallas_call(
        sum_large_kernel,
        out_shape=jax.ShapeDtypeStruct(terms.shape[1:], terms.dtype),
        in_specs=[pl.BlockSpec(memory_space=pltpu.HBM)],
        out_specs=pl.BlockSpec(memory_space=pltpu.VMEM),
        scratch_shapes=[pltpu.VMEM(terms.shape, terms.dtype), pltpu.SemaphoreType.DMA((6,))],
        compiler_params=pltpu.CompilerParams(vmem_limit_bytes=VMEM_LIMIT),
    )(terms)


def add_kernel(*refs):
    *terms, total = refs
    last = total.shape[0]
    value = sum(term[term.shape[0] - last :].astype(jnp.float32) for term in terms)
    total[...] = value.astype(jnp.bfloat16)


def add_last(count, *terms):
    return small_call(add_kernel, jax.ShapeDtypeStruct((count,) + terms[0].shape[1:], terms[0].dtype), *terms)


def weight_end_kernel(*refs):
    *terms, up_grad, down_grad = refs
    slots, each = up_grad.shape[:2]
    for s in range(slots):
        for i in range(each):
            up = sum(term[0, 0, s, i].astype(jnp.float32) for term in terms)
            down = sum(term[0, 1, s, i].astype(jnp.float32) for term in terms)
            up_grad[s, i] = jnp.transpose(up).astype(jnp.bfloat16)
            down_grad[s, i] = down.astype(jnp.bfloat16)


def input_end_kernel(terms, input_grad):
    total = terms[0].astype(jnp.float32)
    for i in range(1, terms.shape[0]):
        total += terms[i].astype(jnp.float32)
    input_grad[...] = jnp.transpose(total).astype(jnp.bfloat16)


def core_seq_pairs(partner):
    return [
        (core * N_SEQ + seq, core * N_SEQ + partner(core, seq)) for core in range(N_DP) for seq in range(N_SEQ)
    ]


def local(inputs, out_grad, up_blocks, down_blocks, up_rows, down_cols, slot_count):
    tok, features = inputs.shape
    slots, fan = up_rows.shape
    each = fan // (N_DP * N_SEQ)
    bf16 = jnp.bfloat16
    smem = pl.BlockSpec(memory_space=pltpu.SMEM)
    vmem = pl.BlockSpec(memory_space=pltpu.VMEM)
    hbm = pl.BlockSpec(memory_space=pltpu.HBM)
    core = lax.axis_index("dp").astype(jnp.int32)
    seq = lax.axis_index("seq").astype(jnp.int32)
    wide = (slots, fan * BLK, BLK)
    placed, hidden_t, pre_grad_t = pl.pallas_call(
        forward_kernel,
        out_shape=(
            jax.ShapeDtypeStruct((N_Y * N_Z, BLK, tok), bf16),
            jax.ShapeDtypeStruct((slots, BLK, tok), bf16),
            jax.ShapeDtypeStruct((slots, BLK, tok), bf16),
        ),
        in_specs=[smem] + [hbm] * 8,
        out_specs=(hbm, vmem, vmem),
        scratch_shapes=[
            pltpu.VMEM((N_Y * N_Z, BLK, tok), bf16),
            pltpu.VMEM((tok, features), bf16),
            pltpu.VMEM((tok, features), bf16),
            pltpu.VMEM(wide, bf16),
            pltpu.VMEM(wide, bf16),
            pltpu.SMEM((N_DP, N_Y * N_Z), jnp.int32),
            pltpu.SMEM((slots, fan), jnp.int32),
            pltpu.SMEM((slots, fan), jnp.int32),
            pltpu.SMEM((1,), jnp.int32),
            pltpu.SemaphoreType.DMA((4,)),
            pltpu.SemaphoreType.DMA((6,)),
            pltpu.SemaphoreType.DMA(()),
        ],
        compiler_params=pltpu.CompilerParams(vmem_limit_bytes=VMEM_LIMIT),
    )(
        core.reshape(1),
        jnp.asarray(place_table(), jnp.int32).reshape(N_DP, N_Y * N_Z),
        up_rows,
        down_cols,
        slot_count,
        inputs,
        out_grad,
        up_blocks.reshape(wide),
        down_blocks.reshape(wide),
    )
    everyone = TOKENS_AX + OWNER_AX
    near = lax.all_to_all(
        placed.reshape(4, 24, BLK, tok), everyone, 0, 0, axis_index_groups=owner_groups(neighbours(N_Y, 0, 0), neighbours(N_Z, 0, 0))
    )

    part_shape = jax.ShapeDtypeStruct((2, 2, slots, each, BLK, BLK), bf16)
    theirs_far, theirs_near, mine_far, mine_near = pl.pallas_call(
        weight_kernel,
        out_shape=(part_shape,) * 4,
        in_specs=[smem] * 4 + [hbm] * 2 + [vmem] * 2,
        out_specs=(vmem,) * 4,
        scratch_shapes=[
            pltpu.VMEM((2, 4, slots, 2 * each, tok, BLK), bf16),
            pltpu.SemaphoreType.DMA((2, 4)),
        ],
        compiler_params=pltpu.CompilerParams(vmem_limit_bytes=12 * 1024 * 1024),
        cost_estimate=pl.CostEstimate(flops=400_000_000, bytes_accessed=10_000_000, transcendentals=0),
    )(core.reshape(1), seq.reshape(1), up_rows, down_cols, inputs, out_grad, hidden_t, pre_grad_t)
    other_core = [(0, 1), (1, 0)]
    far_arrived = lax.ppermute(theirs_far, "dp", other_core)
    near_arrived = lax.ppermute(theirs_near, "dp", other_core)
    first_got = lax.ppermute(
        add_last(2, mine_far, far_arrived), TOKENS_AX, core_seq_pairs(lambda c, q: 3 - q if c else q ^ 1)
    )
    near, _, _ = lax.optimization_barrier((near, far_arrived, near_arrived))
    mid = lax.all_to_all(
        sum_large(near).reshape(4, 6, BLK, tok),
        everyone,
        0,
        0,
        axis_index_groups=owner_groups(neighbours(N_Y, 1, 1), neighbours(N_Z, 1, 1)),
    )
    second_got = lax.ppermute(
        add_last(1, mine_near, near_arrived, first_got),
        TOKENS_AX,
        core_seq_pairs(lambda c, q: q ^ 1 if c else 3 - q),
    )
    far = lax.all_to_all(sum_first(mid), everyone, 0, 0, axis_index_groups=owner_groups(FAR_Y, FAR_Z))

    grad_shape = jax.ShapeDtypeStruct((slots, each, BLK, BLK), bf16)
    up_grad, down_grad = small_call(
        weight_end_kernel, (grad_shape, grad_shape), mine_near, near_arrived, first_got, second_got
    )
    input_grad = small_call(input_end_kernel, jax.ShapeDtypeStruct((tok, BLK), bf16), far)
    return input_grad, up_grad, down_grad


def solution(mesh):
    split = Mesh(mesh.devices.reshape(N_DP, N_SEQ, N_Y, N_Z), TOKENS_AX + OWNER_AX)
    in_specs = (
        P(TOKENS_AX, None),
        P(TOKENS_AX, None),
        P(OWNER_AX, None, None, None),
        P(OWNER_AX, None, None, None),
        P(OWNER_AX, None),
        P(OWNER_AX, None),
        P(OWNER_AX),
    )
    out_specs = (
        P(TOKENS_AX, OWNER_AX),
        P(OWNER_AX, TOKENS_AX, None, None),
        P(OWNER_AX, TOKENS_AX, None, None),
    )
    return jax.shard_map(local, mesh=split, in_specs=in_specs, out_specs=out_specs, check_vma=False)
```

```python
import jax
import jax.numpy as jnp
from jax import lax
from jax.experimental import pallas as pl
from jax.experimental.pallas import tpu as pltpu
from jax.sharding import Mesh
from jax.sharding import PartitionSpec as P

BLK = 128
VMEM_LIMIT = 60 * 1024 * 1024
N_DP, N_SEQ, N_Y, N_Z = 2, 4, 8, 12
TOKENS_AX = ("dp", "seq")
OWNER_AX = ("y", "z")


def gelu_pair(pre_act):
    squared = pre_act * pre_act
    tangent = jnp.tanh(0.7978845608 * (pre_act + 0.044715 * squared * pre_act))
    value = 0.5 * pre_act * (1.0 + tangent)
    slope = 0.5 * (1.0 + tangent) + 0.5 * pre_act * (1.0 - tangent * tangent) * 0.7978845608 * (
        1.0 + 3.0 * 0.044715 * squared
    )
    return value, slope


def two_blocks(ref, first, second):
    return jnp.concatenate(
        [
            ref[:, pl.ds(pl.multiple_of(first * BLK, BLK), BLK)],
            ref[:, pl.ds(pl.multiple_of(second * BLK, BLK), BLK)],
        ],
        axis=1,
    )


def fetch_columns(source, indices, target, sem):
    for i, index in enumerate(indices):
        columns = source.at[:, pl.ds(pl.multiple_of(index * BLK, BLK), BLK)]
        pltpu.make_async_copy(columns, target.at[i], sem).start()


def wait_for(target, sem):
    pltpu.make_async_copy(target, target, sem).wait()


def dot_nn(left, right):
    return lax.dot_general(left, right, (((1,), (0,)), ((), ())), preferred_element_type=jnp.float32)


def dot_nt(left, right):
    return lax.dot_general(left, right, (((1,), (1,)), ((), ())), preferred_element_type=jnp.float32)


def ring_place(size, far_groups):
    first = [0 if p % 4 in (0, 3) else 1 for p in range(size)]
    third = {p: group.index(p) for group in far_groups for p in group}
    second = {}
    for group in far_groups:
        for p in group:
            second[p] = 0 if min(group) in (0, 1) else 1
    return [(first[p], second[p], third[p]) for p in range(size)]


FAR_Y = [[0, 3], [1, 6], [2, 5], [4, 7]]
FAR_Z = [[p, p + 4, p + 8] for p in range(4)]
PLACE_Y, PLACE_Z = ring_place(N_Y, FAR_Y), ring_place(N_Z, FAR_Z)


def place_table():
    table = []
    for core in range(N_DP):
        for r in range(N_Y * N_Z):
            a, b = PLACE_Y[(r // N_Z - core) % N_Y], PLACE_Z[(r % N_Z - core) % N_Z]
            table.append(((a[0] * 2 + b[0]) * 4 + a[1] * 2 + b[1]) * 6 + a[2] * 3 + b[2])
    return table


def owner_groups(groups_y, groups_z):
    return [
        [
            ((core * N_SEQ + seq) * N_Y + (y + core) % N_Y) * N_Z + (z + core) % N_Z
            for y in group_y
            for z in group_z
        ]
        for core in range(N_DP)
        for seq in range(N_SEQ)
        for group_y in groups_y
        for group_z in groups_z
    ]


def neighbours(size, start, step):
    place = PLACE_Y if size == N_Y else PLACE_Z
    return [sorted((p, (p + 1) % size), key=lambda q: place[q][step]) for p in range(start, size, 2)]


def forward_kernel(
    core, place_hbm, rows_hbm, cols_hbm, count_hbm, inputs_hbm, out_grad_hbm, ups_hbm, downs_hbm,
    placed_hbm, hidden_t_hbm, pre_grad_t_hbm,
    placed, hidden_t, pre_grad_t, inputs, out_grad, ups, downs, place, rows, cols, count, small_sems, sems, out_sems,
):
    slots, fan = rows.shape
    tok = inputs.shape[0]
    half = BLK // 2

    def copies_of(pairs, semaphores):
        return [pltpu.make_async_copy(a, b, semaphores.at[i]) for i, (a, b) in enumerate(pairs)]

    small = copies_of(((rows_hbm, rows), (cols_hbm, cols), (place_hbm, place), (count_hbm, count)), small_sems)
    large = copies_of(
        (
            (ups_hbm.at[0], ups.at[0]),
            (inputs_hbm, inputs),
            (ups_hbm.at[1], ups.at[1]),
            (downs_hbm.at[0], downs.at[0]),
            (out_grad_hbm, out_grad),
            (downs_hbm.at[1], downs.at[1]),
        ),
        sems,
    )
    written = copies_of(
        (
            (placed.at[:, pl.ds(0, half)], placed_hbm.at[:, pl.ds(0, half)]),
            (placed.at[:, pl.ds(half, half)], placed_hbm.at[:, pl.ds(half, half)]),
            (hidden_t, hidden_t_hbm),
            (pre_grad_t, pre_grad_t_hbm),
        ),
        out_sems,
    )
    for copy in small + large:
        copy.start()
    placed[...] = jnp.zeros_like(placed)
    for copy in small:
        copy.wait()
    slopes = []
    for s in range(slots):
        live = (s < count[0]).astype(jnp.float32)
        for copy in large[:2] if s == 0 else large[2:3]:
            copy.wait()
        pre_act = jnp.zeros((tok, BLK), jnp.float32)
        for k in range(0, fan, 2):
            pre_act += dot_nn(two_blocks(inputs, rows[s, k], rows[s, k + 1]), ups[s, k * BLK : (k + 2) * BLK, :])
        value, slope = gelu_pair(pre_act)
        hidden_t[s] = jnp.transpose(value * live).astype(jnp.bfloat16)
        slopes.append(slope * live)
    written[2].start()
    for s in range(slots):
        for copy in large[3:5] if s == 0 else large[5:]:
            copy.wait()
        hid_grad = jnp.zeros((tok, BLK), jnp.float32)
        for k in range(0, fan, 2):
            hid_grad += dot_nt(
                two_blocks(out_grad, cols[s, k], cols[s, k + 1]),
                jnp.concatenate([downs[s, k * BLK : (k + 1) * BLK, :], downs[s, (k + 1) * BLK : (k + 2) * BLK, :]], axis=1),
            )
        pre_grad_t[s] = jnp.transpose(hid_grad * slopes[s]).astype(jnp.bfloat16)
    written[3].start()
    for h in range(2):
        part = slice(h * half, (h + 1) * half)
        for s in range(slots):
            turned = pre_grad_t[s]
            for k in range(0, fan, 2):
                edges = [(k + i) * BLK + h * half for i in range(2)]
                both = dot_nn(jnp.concatenate([ups[s, e : e + half, :] for e in edges], axis=0), turned)
                for i in range(2):
                    at = place[core[0], rows[s, k + i]]
                    product = both[i * half : (i + 1) * half, :]
                    if s > 0:
                        product += placed[at, part].astype(jnp.float32)
                    placed[at, part] = product.astype(jnp.bfloat16)
        written[h].start()
    for copy in written:
        copy.wait()


def weight_kernel(
    core, seq, rows, cols, inputs, out_grad,
    hidden_t, pre_grad_t, theirs_far, theirs_near, mine_far, mine_near, fetched, sems,
):
    slots = rows.shape[0]
    parts, each = mine_far.shape[0], mine_far.shape[3]
    here, there = core[0] * N_SEQ, (1 - core[0]) * N_SEQ
    flip, mirror, across = seq[0] ^ 1, 3 - seq[0], seq[0] ^ 2
    first = jnp.where(core[0] == 0, flip, mirror)
    second = flip + mirror - first
    targets = (
        (theirs_far, (there + second, there + across)),
        (theirs_near, (there + seq[0], there + first)),
        (mine_far, (here + first, here + across)),
        (mine_near, (here + seq[0], here + second)),
    )
    for half, (data, ids) in enumerate(((inputs, rows), (out_grad, cols))):
        for t, (_, groups) in enumerate(targets):
            for s in range(slots):
                ks = [group * each + i for group in groups for i in range(each)]
                fetch_columns(data, [ids[s, k] for k in ks], fetched.at[half, t, s], sems.at[half, t])
    for half, left in enumerate((pre_grad_t, hidden_t)):
        for t, (target, _) in enumerate(targets):
            wait_for(fetched.at[half, t], sems.at[half, t])
            for s in range(slots):
                for j in range(0, parts * each, 2):
                    pair = jnp.concatenate([fetched[half, t, s, j], fetched[half, t, s, j + 1]], axis=1)
                    both = dot_nn(left[s], pair)
                    for i in range(2):
                        value = both[:, i * BLK : (i + 1) * BLK]
                        target[(j + i) // each, half, s, (j + i) % each] = value.astype(jnp.bfloat16)


def small_call(kernel, out_shape, *operands):
    vmem = pl.BlockSpec(memory_space=pltpu.VMEM)
    return pl.pallas_call(
        kernel,
        out_shape=out_shape,
        in_specs=[vmem] * len(operands),
        out_specs=jax.tree.map(lambda _: vmem, out_shape),
        compiler_params=pltpu.CompilerParams(vmem_limit_bytes=8 * 1024 * 1024),
    )(*operands)


def sum_first_kernel(terms, total):
    value = terms[0].astype(jnp.float32)
    for i in range(1, terms.shape[0]):
        value += terms[i].astype(jnp.float32)
    total[...] = value.astype(jnp.bfloat16)


def sum_first(terms):
    return small_call(sum_first_kernel, jax.ShapeDtypeStruct(terms.shape[1:], terms.dtype), terms)


def sum_large_kernel(terms_hbm, total_hbm, terms, total, sems, out_sems):
    edges = [0, 6, 12, 17, 21, 24]
    pieces = [pl.ds(a, b - a) for a, b in zip(edges, edges[1:])]
    copies = [
        pltpu.make_async_copy(terms_hbm.at[:, piece], terms.at[:, piece], sems.at[i])
        for i, piece in enumerate(pieces)
    ]
    written = [
        pltpu.make_async_copy(total.at[piece], total_hbm.at[piece], out_sems.at[i])
        for i, piece in enumerate(pieces)
    ]
    for copy in copies:
        copy.start()
    for copy, write, piece in zip(copies, written, pieces):
        copy.wait()
        value = terms[0, piece].astype(jnp.float32)
        for i in range(1, terms.shape[0]):
            value += terms[i, piece].astype(jnp.float32)
        total[piece] = value.astype(jnp.bfloat16)
        write.start()
    for write in written:
        write.wait()


def sum_large(terms):
    hbm = pl.BlockSpec(memory_space=pltpu.HBM)
    return pl.pallas_call(
        sum_large_kernel,
        out_shape=jax.ShapeDtypeStruct(terms.shape[1:], terms.dtype),
        in_specs=[hbm],
        out_specs=hbm,
        scratch_shapes=[
            pltpu.VMEM(terms.shape, terms.dtype),
            pltpu.VMEM(terms.shape[1:], terms.dtype),
            pltpu.SemaphoreType.DMA((5,)),
            pltpu.SemaphoreType.DMA((5,)),
        ],
        compiler_params=pltpu.CompilerParams(vmem_limit_bytes=VMEM_LIMIT),
    )(terms)


def add_kernel(*refs):
    *terms, total = refs
    last = total.shape[0]
    value = sum(term[term.shape[0] - last :].astype(jnp.float32) for term in terms)
    total[...] = value.astype(jnp.bfloat16)


def add_last(count, *terms):
    return small_call(add_kernel, jax.ShapeDtypeStruct((count,) + terms[0].shape[1:], terms[0].dtype), *terms)


def weight_end_kernel(*refs):
    *terms, up_grad, down_grad = refs
    slots, each = up_grad.shape[:2]
    for s in range(slots):
        for i in range(each):
            up = sum(term[0, 0, s, i].astype(jnp.float32) for term in terms)
            down = sum(term[0, 1, s, i].astype(jnp.float32) for term in terms)
            up_grad[s, i] = jnp.transpose(up).astype(jnp.bfloat16)
            down_grad[s, i] = down.astype(jnp.bfloat16)


def input_end_kernel(terms, input_grad):
    total = terms[0].astype(jnp.float32)
    for i in range(1, terms.shape[0]):
        total += terms[i].astype(jnp.float32)
    input_grad[...] = jnp.transpose(total).astype(jnp.bfloat16)


def core_seq_pairs(partner):
    return [
        (core * N_SEQ + seq, core * N_SEQ + partner(core, seq)) for core in range(N_DP) for seq in range(N_SEQ)
    ]


def local(inputs, out_grad, up_blocks, down_blocks, up_rows, down_cols, slot_count):
    tok, features = inputs.shape
    slots, fan = up_rows.shape
    each = fan // (N_DP * N_SEQ)
    bf16 = jnp.bfloat16
    smem = pl.BlockSpec(memory_space=pltpu.SMEM)
    vmem = pl.BlockSpec(memory_space=pltpu.VMEM)
    hbm = pl.BlockSpec(memory_space=pltpu.HBM)
    core = lax.axis_index("dp").astype(jnp.int32)
    seq = lax.axis_index("seq").astype(jnp.int32)
    wide = (slots, fan * BLK, BLK)
    placed, hidden_t, pre_grad_t = pl.pallas_call(
        forward_kernel,
        out_shape=(
            jax.ShapeDtypeStruct((N_Y * N_Z, BLK, tok), bf16),
            jax.ShapeDtypeStruct((slots, BLK, tok), bf16),
            jax.ShapeDtypeStruct((slots, BLK, tok), bf16),
        ),
        in_specs=[smem] + [hbm] * 8,
        out_specs=(hbm,) * 3,
        scratch_shapes=[
            pltpu.VMEM((N_Y * N_Z, BLK, tok), bf16),
            pltpu.VMEM((slots, BLK, tok), bf16),
            pltpu.VMEM((slots, BLK, tok), bf16),
            pltpu.VMEM((tok, features), bf16),
            pltpu.VMEM((tok, features), bf16),
            pltpu.VMEM(wide, bf16),
            pltpu.VMEM(wide, bf16),
            pltpu.SMEM((N_DP, N_Y * N_Z), jnp.int32),
            pltpu.SMEM((slots, fan), jnp.int32),
            pltpu.SMEM((slots, fan), jnp.int32),
            pltpu.SMEM((1,), jnp.int32),
            pltpu.SemaphoreType.DMA((4,)),
            pltpu.SemaphoreType.DMA((6,)),
            pltpu.SemaphoreType.DMA((4,)),
        ],
        compiler_params=pltpu.CompilerParams(vmem_limit_bytes=VMEM_LIMIT),
    )(
        core.reshape(1),
        jnp.asarray(place_table(), jnp.int32).reshape(N_DP, N_Y * N_Z),
        up_rows,
        down_cols,
        slot_count,
        inputs,
        out_grad,
        up_blocks.reshape(wide),
        down_blocks.reshape(wide),
    )
    everyone = TOKENS_AX + OWNER_AX
    near = lax.all_to_all(
        placed.reshape(4, 24, BLK, tok), everyone, 0, 0, axis_index_groups=owner_groups(neighbours(N_Y, 0, 0), neighbours(N_Z, 0, 0))
    )

    part_shape = jax.ShapeDtypeStruct((2, 2, slots, each, BLK, BLK), bf16)
    theirs_far, theirs_near, mine_far, mine_near = pl.pallas_call(
        weight_kernel,
        out_shape=(part_shape,) * 4,
        in_specs=[smem] * 4 + [hbm] * 2 + [vmem] * 2,
        out_specs=(vmem,) * 4,
        scratch_shapes=[
            pltpu.VMEM((2, 4, slots, 2 * each, tok, BLK), bf16),
            pltpu.SemaphoreType.DMA((2, 4)),
        ],
        compiler_params=pltpu.CompilerParams(vmem_limit_bytes=12 * 1024 * 1024),
        cost_estimate=pl.CostEstimate(flops=400_000_000, bytes_accessed=10_000_000, transcendentals=0),
    )(core.reshape(1), seq.reshape(1), up_rows, down_cols, inputs, out_grad, hidden_t, pre_grad_t)
    other_core = [(0, 1), (1, 0)]
    far_arrived = lax.ppermute(theirs_far, "dp", other_core)
    near_arrived = lax.ppermute(theirs_near, "dp", other_core)
    first_sent = add_last(2, mine_far, far_arrived)
    first_got = lax.ppermute(first_sent, TOKENS_AX, core_seq_pairs(lambda c, q: 3 - q if c else q ^ 1))
    near, _, _ = lax.optimization_barrier((near, first_sent, near_arrived))
    mid = lax.all_to_all(
        sum_large(near).reshape(4, 6, BLK, tok),
        everyone,
        0,
        0,
        axis_index_groups=owner_groups(neighbours(N_Y, 1, 1), neighbours(N_Z, 1, 1)),
    )
    second_got = lax.ppermute(
        add_last(1, mine_near, near_arrived, first_got),
        TOKENS_AX,
        core_seq_pairs(lambda c, q: q ^ 1 if c else 3 - q),
    )
    far = lax.all_to_all(sum_first(mid), everyone, 0, 0, axis_index_groups=owner_groups(FAR_Y, FAR_Z))

    grad_shape = jax.ShapeDtypeStruct((slots, each, BLK, BLK), bf16)
    up_grad, down_grad = small_call(
        weight_end_kernel, (grad_shape, grad_shape), mine_near, near_arrived, first_got, second_got
    )
    input_grad = small_call(input_end_kernel, jax.ShapeDtypeStruct((tok, BLK), bf16), far)
    return input_grad, up_grad, down_grad


def solution(mesh):
    split = Mesh(mesh.devices.reshape(N_DP, N_SEQ, N_Y, N_Z), TOKENS_AX + OWNER_AX)
    in_specs = (
        P(TOKENS_AX, None),
        P(TOKENS_AX, None),
        P(OWNER_AX, None, None, None),
        P(OWNER_AX, None, None, None),
        P(OWNER_AX, None),
        P(OWNER_AX, None),
        P(OWNER_AX),
    )
    out_specs = (
        P(TOKENS_AX, OWNER_AX),
        P(OWNER_AX, TOKENS_AX, None, None),
        P(OWNER_AX, TOKENS_AX, None, None),
    )
    return jax.shard_map(local, mesh=split, in_specs=in_specs, out_specs=out_specs, check_vma=False)
```

```python
import jax
import jax.numpy as jnp
from jax import lax
from jax.experimental import pallas as pl
from jax.experimental.pallas import tpu as pltpu
from jax.sharding import Mesh
from jax.sharding import PartitionSpec as P

BLK = 128
VMEM_LIMIT = 60 * 1024 * 1024
N_DP, N_SEQ, N_Y, N_Z = 2, 4, 8, 12
TOKENS_AX = ("dp", "seq")
OWNER_AX = ("y", "z")


def gelu_pair(pre_act):
    squared = pre_act * pre_act
    tangent = jnp.tanh(0.7978845608 * (pre_act + 0.044715 * squared * pre_act))
    value = 0.5 * pre_act * (1.0 + tangent)
    slope = 0.5 * (1.0 + tangent) + 0.5 * pre_act * (1.0 - tangent * tangent) * 0.7978845608 * (
        1.0 + 3.0 * 0.044715 * squared
    )
    return value, slope


def two_blocks(ref, first, second):
    return jnp.concatenate(
        [
            ref[:, pl.ds(pl.multiple_of(first * BLK, BLK), BLK)],
            ref[:, pl.ds(pl.multiple_of(second * BLK, BLK), BLK)],
        ],
        axis=1,
    )


def fetch_columns(source, indices, target, sem):
    for i, index in enumerate(indices):
        columns = source.at[:, pl.ds(pl.multiple_of(index * BLK, BLK), BLK)]
        pltpu.make_async_copy(columns, target.at[i], sem).start()


def wait_for(target, sem):
    pltpu.make_async_copy(target, target, sem).wait()


def dot_nn(left, right):
    return lax.dot_general(left, right, (((1,), (0,)), ((), ())), preferred_element_type=jnp.float32)


def dot_nt(left, right):
    return lax.dot_general(left, right, (((1,), (1,)), ((), ())), preferred_element_type=jnp.float32)


def ring_place(size, far_groups):
    first = [0 if p % 4 in (0, 3) else 1 for p in range(size)]
    third = {p: group.index(p) for group in far_groups for p in group}
    second = {}
    for group in far_groups:
        for p in group:
            second[p] = 0 if min(group) in (0, 1) else 1
    return [(first[p], second[p], third[p]) for p in range(size)]


FAR_Y = [[0, 3], [1, 6], [2, 5], [4, 7]]
FAR_Z = [[p, p + 4, p + 8] for p in range(4)]
PLACE_Y, PLACE_Z = ring_place(N_Y, FAR_Y), ring_place(N_Z, FAR_Z)


def place_table():
    table = []
    for core in range(N_DP):
        for r in range(N_Y * N_Z):
            a, b = PLACE_Y[(r // N_Z - core) % N_Y], PLACE_Z[(r % N_Z - core) % N_Z]
            table.append(((a[0] * 2 + b[0]) * 4 + a[1] * 2 + b[1]) * 6 + a[2] * 3 + b[2])
    return table


def owner_groups(groups_y, groups_z):
    return [
        [
            ((core * N_SEQ + seq) * N_Y + (y + core) % N_Y) * N_Z + (z + core) % N_Z
            for y in group_y
            for z in group_z
        ]
        for core in range(N_DP)
        for seq in range(N_SEQ)
        for group_y in groups_y
        for group_z in groups_z
    ]


def neighbours(size, start, step):
    place = PLACE_Y if size == N_Y else PLACE_Z
    return [sorted((p, (p + 1) % size), key=lambda q: place[q][step]) for p in range(start, size, 2)]


def forward_kernel(
    core, place_hbm, rows_hbm, cols_hbm, count_hbm, inputs_hbm, out_grad_hbm, ups_hbm, downs_hbm,
    placed_hbm, hidden_t_hbm, pre_grad_t_hbm,
    placed, hidden_t, pre_grad_t, inputs, out_grad, ups, downs, place, rows, cols, count, small_sems, sems, out_sems,
):
    slots, fan = rows.shape
    tok = inputs.shape[0]
    quarter = BLK // 4

    def copies_of(pairs, semaphores):
        return [pltpu.make_async_copy(a, b, semaphores.at[i]) for i, (a, b) in enumerate(pairs)]

    small = copies_of(((rows_hbm, rows), (cols_hbm, cols), (place_hbm, place), (count_hbm, count)), small_sems)
    large = copies_of(
        (
            (inputs_hbm, inputs),
            (ups_hbm.at[0], ups.at[0]),
            (ups_hbm.at[1], ups.at[1]),
            (out_grad_hbm, out_grad),
            (downs_hbm.at[0], downs.at[0]),
            (downs_hbm.at[1], downs.at[1]),
        ),
        sems,
    )
    written = copies_of(
        [(placed.at[:, pl.ds(h * quarter, quarter)], placed_hbm.at[:, pl.ds(h * quarter, quarter)]) for h in range(4)]
        + [(hidden_t, hidden_t_hbm), (pre_grad_t, pre_grad_t_hbm)],
        out_sems,
    )
    for copy in small + large:
        copy.start()
    placed[...] = jnp.zeros_like(placed)
    for copy in small:
        copy.wait()
    slopes = []
    for s in range(slots):
        live = (s < count[0]).astype(jnp.float32)
        for copy in large[:2] if s == 0 else large[2:3]:
            copy.wait()
        pre_act = jnp.zeros((tok, BLK), jnp.float32)
        for k in range(0, fan, 2):
            pre_act += dot_nn(two_blocks(inputs, rows[s, k], rows[s, k + 1]), ups[s, k * BLK : (k + 2) * BLK, :])
        value, slope = gelu_pair(pre_act)
        hidden_t[s] = jnp.transpose(value * live).astype(jnp.bfloat16)
        slopes.append(slope * live)
    written[4].start()
    for s in range(slots):
        for copy in large[3:5] if s == 0 else large[5:]:
            copy.wait()
        hid_grad = jnp.zeros((tok, BLK), jnp.float32)
        for k in range(0, fan, 2):
            hid_grad += dot_nt(
                two_blocks(out_grad, cols[s, k], cols[s, k + 1]),
                jnp.concatenate([downs[s, k * BLK : (k + 1) * BLK, :], downs[s, (k + 1) * BLK : (k + 2) * BLK, :]], axis=1),
            )
        pre_grad_t[s] = jnp.transpose(hid_grad * slopes[s]).astype(jnp.bfloat16)
    written[5].start()
    for h in range(4):
        part = slice(h * quarter, (h + 1) * quarter)
        for s in range(slots):
            turned = pre_grad_t[s]
            for k in range(0, fan, 4):
                edges = [(k + i) * BLK + h * quarter for i in range(4)]
                both = dot_nn(jnp.concatenate([ups[s, e : e + quarter, :] for e in edges], axis=0), turned)
                for i in range(4):
                    at = place[core[0], rows[s, k + i]]
                    product = both[i * quarter : (i + 1) * quarter, :]
                    if s > 0:
                        product += placed[at, part].astype(jnp.float32)
                    placed[at, part] = product.astype(jnp.bfloat16)
        written[h].start()
    for copy in written:
        copy.wait()


def weight_kernel(
    core, seq, rows, cols, inputs, out_grad,
    hidden_t, pre_grad_t, theirs_far, theirs_near, mine_far, mine_near, fetched, sems,
):
    slots = rows.shape[0]
    parts, each = mine_far.shape[0], mine_far.shape[3]
    here, there = core[0] * N_SEQ, (1 - core[0]) * N_SEQ
    flip, mirror, across = seq[0] ^ 1, 3 - seq[0], seq[0] ^ 2
    first = jnp.where(core[0] == 0, flip, mirror)
    second = flip + mirror - first
    targets = (
        (theirs_far, (there + second, there + across)),
        (theirs_near, (there + seq[0], there + first)),
        (mine_far, (here + first, here + across)),
        (mine_near, (here + seq[0], here + second)),
    )
    for half, (data, ids) in enumerate(((inputs, rows), (out_grad, cols))):
        for t, (_, groups) in enumerate(targets):
            for s in range(slots):
                ks = [group * each + i for group in groups for i in range(each)]
                fetch_columns(data, [ids[s, k] for k in ks], fetched.at[half, t, s], sems.at[half, t])
    for half, left in enumerate((pre_grad_t, hidden_t)):
        for t, (target, _) in enumerate(targets):
            wait_for(fetched.at[half, t], sems.at[half, t])
            for s in range(slots):
                for j in range(0, parts * each, 2):
                    pair = jnp.concatenate([fetched[half, t, s, j], fetched[half, t, s, j + 1]], axis=1)
                    both = dot_nn(left[s], pair)
                    for i in range(2):
                        value = both[:, i * BLK : (i + 1) * BLK]
                        target[(j + i) // each, half, s, (j + i) % each] = value.astype(jnp.bfloat16)


def small_call(kernel, out_shape, *operands):
    vmem = pl.BlockSpec(memory_space=pltpu.VMEM)
    return pl.pallas_call(
        kernel,
        out_shape=out_shape,
        in_specs=[vmem] * len(operands),
        out_specs=jax.tree.map(lambda _: vmem, out_shape),
        compiler_params=pltpu.CompilerParams(vmem_limit_bytes=8 * 1024 * 1024),
    )(*operands)


def sum_first_kernel(terms, total):
    value = terms[0].astype(jnp.float32)
    for i in range(1, terms.shape[0]):
        value += terms[i].astype(jnp.float32)
    total[...] = value.astype(jnp.bfloat16)


def sum_first(terms):
    return small_call(sum_first_kernel, jax.ShapeDtypeStruct(terms.shape[1:], terms.dtype), terms)


def sum_large_kernel(terms_hbm, total_hbm, terms, total, sems, out_sems):
    edges = [0, 6, 12, 17, 21, 24]
    pieces = [pl.ds(a, b - a) for a, b in zip(edges, edges[1:])]
    copies = [
        pltpu.make_async_copy(terms_hbm.at[:, piece], terms.at[:, piece], sems.at[i])
        for i, piece in enumerate(pieces)
    ]
    written = [
        pltpu.make_async_copy(total.at[piece], total_hbm.at[piece], out_sems.at[i])
        for i, piece in enumerate(pieces)
    ]
    for copy in copies:
        copy.start()
    for copy, write, piece in zip(copies, written, pieces):
        copy.wait()
        value = terms[0, piece].astype(jnp.float32)
        for i in range(1, terms.shape[0]):
            value += terms[i, piece].astype(jnp.float32)
        total[piece] = value.astype(jnp.bfloat16)
        write.start()
    for write in written:
        write.wait()


def sum_large(terms):
    hbm = pl.BlockSpec(memory_space=pltpu.HBM)
    return pl.pallas_call(
        sum_large_kernel,
        out_shape=jax.ShapeDtypeStruct(terms.shape[1:], terms.dtype),
        in_specs=[hbm],
        out_specs=hbm,
        scratch_shapes=[
            pltpu.VMEM(terms.shape, terms.dtype),
            pltpu.VMEM(terms.shape[1:], terms.dtype),
            pltpu.SemaphoreType.DMA((5,)),
            pltpu.SemaphoreType.DMA((5,)),
        ],
        compiler_params=pltpu.CompilerParams(vmem_limit_bytes=VMEM_LIMIT),
    )(terms)


def add_kernel(*refs):
    *terms, total = refs
    last = total.shape[0]
    value = sum(term[term.shape[0] - last :].astype(jnp.float32) for term in terms)
    total[...] = value.astype(jnp.bfloat16)


def add_last(count, *terms):
    return small_call(add_kernel, jax.ShapeDtypeStruct((count,) + terms[0].shape[1:], terms[0].dtype), *terms)


def weight_end_kernel(*refs):
    *terms, up_grad, down_grad = refs
    slots, each = up_grad.shape[:2]
    for s in range(slots):
        for i in range(each):
            up = sum(term[0, 0, s, i].astype(jnp.float32) for term in terms)
            down = sum(term[0, 1, s, i].astype(jnp.float32) for term in terms)
            up_grad[s, i] = jnp.transpose(up).astype(jnp.bfloat16)
            down_grad[s, i] = down.astype(jnp.bfloat16)


def input_end_kernel(terms, input_grad):
    total = terms[0].astype(jnp.float32)
    for i in range(1, terms.shape[0]):
        total += terms[i].astype(jnp.float32)
    input_grad[...] = jnp.transpose(total).astype(jnp.bfloat16)


def core_seq_pairs(partner):
    return [
        (core * N_SEQ + seq, core * N_SEQ + partner(core, seq)) for core in range(N_DP) for seq in range(N_SEQ)
    ]


def local(inputs, out_grad, up_blocks, down_blocks, up_rows, down_cols, slot_count):
    tok, features = inputs.shape
    slots, fan = up_rows.shape
    each = fan // (N_DP * N_SEQ)
    bf16 = jnp.bfloat16
    smem = pl.BlockSpec(memory_space=pltpu.SMEM)
    vmem = pl.BlockSpec(memory_space=pltpu.VMEM)
    hbm = pl.BlockSpec(memory_space=pltpu.HBM)
    core = lax.axis_index("dp").astype(jnp.int32)
    seq = lax.axis_index("seq").astype(jnp.int32)
    wide = (slots, fan * BLK, BLK)
    placed, hidden_t, pre_grad_t = pl.pallas_call(
        forward_kernel,
        out_shape=(
            jax.ShapeDtypeStruct((N_Y * N_Z, BLK, tok), bf16),
            jax.ShapeDtypeStruct((slots, BLK, tok), bf16),
            jax.ShapeDtypeStruct((slots, BLK, tok), bf16),
        ),
        in_specs=[smem] + [hbm] * 8,
        out_specs=(hbm,) * 3,
        scratch_shapes=[
            pltpu.VMEM((N_Y * N_Z, BLK, tok), bf16),
            pltpu.VMEM((slots, BLK, tok), bf16),
            pltpu.VMEM((slots, BLK, tok), bf16),
            pltpu.VMEM((tok, features), bf16),
            pltpu.VMEM((tok, features), bf16),
            pltpu.VMEM(wide, bf16),
            pltpu.VMEM(wide, bf16),
            pltpu.SMEM((N_DP, N_Y * N_Z), jnp.int32),
            pltpu.SMEM((slots, fan), jnp.int32),
            pltpu.SMEM((slots, fan), jnp.int32),
            pltpu.SMEM((1,), jnp.int32),
            pltpu.SemaphoreType.DMA((4,)),
            pltpu.SemaphoreType.DMA((6,)),
            pltpu.SemaphoreType.DMA((6,)),
        ],
        compiler_params=pltpu.CompilerParams(vmem_limit_bytes=VMEM_LIMIT),
    )(
        core.reshape(1),
        jnp.asarray(place_table(), jnp.int32).reshape(N_DP, N_Y * N_Z),
        up_rows,
        down_cols,
        slot_count,
        inputs,
        out_grad,
        up_blocks.reshape(wide),
        down_blocks.reshape(wide),
    )
    everyone = TOKENS_AX + OWNER_AX
    near = lax.all_to_all(
        placed.reshape(4, 24, BLK, tok), everyone, 0, 0, axis_index_groups=owner_groups(neighbours(N_Y, 0, 0), neighbours(N_Z, 0, 0))
    )

    part_shape = jax.ShapeDtypeStruct((2, 2, slots, each, BLK, BLK), bf16)
    theirs_far, theirs_near, mine_far, mine_near = pl.pallas_call(
        weight_kernel,
        out_shape=(part_shape,) * 4,
        in_specs=[smem] * 4 + [hbm] * 2 + [vmem] * 2,
        out_specs=(vmem,) * 4,
        scratch_shapes=[
            pltpu.VMEM((2, 4, slots, 2 * each, tok, BLK), bf16),
            pltpu.SemaphoreType.DMA((2, 4)),
        ],
        compiler_params=pltpu.CompilerParams(vmem_limit_bytes=12 * 1024 * 1024),
        cost_estimate=pl.CostEstimate(flops=400_000_000, bytes_accessed=10_000_000, transcendentals=0),
    )(core.reshape(1), seq.reshape(1), up_rows, down_cols, inputs, out_grad, hidden_t, pre_grad_t)
    other_core = [(0, 1), (1, 0)]
    far_arrived = lax.ppermute(theirs_far, "dp", other_core)
    near_arrived = lax.ppermute(theirs_near, "dp", other_core)
    first_sent = add_last(2, mine_far, far_arrived)
    first_got = lax.ppermute(first_sent, TOKENS_AX, core_seq_pairs(lambda c, q: 3 - q if c else q ^ 1))
    near, _, _ = lax.optimization_barrier((near, first_sent, near_arrived))
    mid = lax.all_to_all(
        sum_large(near).reshape(4, 6, BLK, tok),
        everyone,
        0,
        0,
        axis_index_groups=owner_groups(neighbours(N_Y, 1, 1), neighbours(N_Z, 1, 1)),
    )
    second_got = lax.ppermute(
        add_last(1, mine_near, near_arrived, first_got),
        TOKENS_AX,
        core_seq_pairs(lambda c, q: q ^ 1 if c else 3 - q),
    )
    far = lax.all_to_all(sum_first(mid), everyone, 0, 0, axis_index_groups=owner_groups(FAR_Y, FAR_Z))

    grad_shape = jax.ShapeDtypeStruct((slots, each, BLK, BLK), bf16)
    up_grad, down_grad = small_call(
        weight_end_kernel, (grad_shape, grad_shape), mine_near, near_arrived, first_got, second_got
    )
    input_grad = small_call(input_end_kernel, jax.ShapeDtypeStruct((tok, BLK), bf16), far)
    return input_grad, up_grad, down_grad


def solution(mesh):
    split = Mesh(mesh.devices.reshape(N_DP, N_SEQ, N_Y, N_Z), TOKENS_AX + OWNER_AX)
    in_specs = (
        P(TOKENS_AX, None),
        P(TOKENS_AX, None),
        P(OWNER_AX, None, None, None),
        P(OWNER_AX, None, None, None),
        P(OWNER_AX, None),
        P(OWNER_AX, None),
        P(OWNER_AX),
    )
    out_specs = (
        P(TOKENS_AX, OWNER_AX),
        P(OWNER_AX, TOKENS_AX, None, None),
        P(OWNER_AX, TOKENS_AX, None, None),
    )
    return jax.shard_map(local, mesh=split, in_specs=in_specs, out_specs=out_specs, check_vma=False)
```

```python
import jax
import jax.numpy as jnp
from jax import lax
from jax.experimental import pallas as pl
from jax.experimental.pallas import tpu as pltpu
from jax.sharding import Mesh
from jax.sharding import PartitionSpec as P

BLK = 128
VMEM_LIMIT = 60 * 1024 * 1024
N_DP, N_SEQ, N_Y, N_Z = 2, 4, 8, 12
TOKENS_AX = ("dp", "seq")
OWNER_AX = ("y", "z")


def gelu_pair(pre_act):
    squared = pre_act * pre_act
    tangent = jnp.tanh(0.7978845608 * (pre_act + 0.044715 * squared * pre_act))
    value = 0.5 * pre_act * (1.0 + tangent)
    slope = 0.5 * (1.0 + tangent) + 0.5 * pre_act * (1.0 - tangent * tangent) * 0.7978845608 * (
        1.0 + 3.0 * 0.044715 * squared
    )
    return value, slope


def two_blocks(ref, first, second):
    return jnp.concatenate(
        [
            ref[:, pl.ds(pl.multiple_of(first * BLK, BLK), BLK)],
            ref[:, pl.ds(pl.multiple_of(second * BLK, BLK), BLK)],
        ],
        axis=1,
    )


def fetch_columns(source, indices, target, sem):
    for i, index in enumerate(indices):
        columns = source.at[:, pl.ds(pl.multiple_of(index * BLK, BLK), BLK)]
        pltpu.make_async_copy(columns, target.at[i], sem).start()


def wait_for(target, sem):
    pltpu.make_async_copy(target, target, sem).wait()


def dot_nn(left, right):
    return lax.dot_general(left, right, (((1,), (0,)), ((), ())), preferred_element_type=jnp.float32)


def dot_nt(left, right):
    return lax.dot_general(left, right, (((1,), (1,)), ((), ())), preferred_element_type=jnp.float32)


def ring_place(size, far_groups):
    first = [0 if p % 4 in (0, 3) else 1 for p in range(size)]
    third = {p: group.index(p) for group in far_groups for p in group}
    second = {}
    for group in far_groups:
        for p in group:
            second[p] = 0 if min(group) in (0, 1) else 1
    return [(first[p], second[p], third[p]) for p in range(size)]


FAR_Y = [[0, 3], [1, 6], [2, 5], [4, 7]]
FAR_Z = [[p, p + 4, p + 8] for p in range(4)]
PLACE_Y, PLACE_Z = ring_place(N_Y, FAR_Y), ring_place(N_Z, FAR_Z)


AROUND = (0, 3, 1, 2)


def around(groups):
    return [[group[i] for i in AROUND] for group in groups]


def place_table():
    table = []
    for core in range(N_DP):
        for r in range(N_Y * N_Z):
            a, b = PLACE_Y[(r // N_Z - core) % N_Y], PLACE_Z[(r % N_Z - core) % N_Z]
            near, mid = AROUND.index(a[0] * 2 + b[0]), AROUND.index(a[1] * 2 + b[1])
            table.append((near * 4 + mid) * 6 + a[2] * 3 + b[2])
    return table


def owner_groups(groups_y, groups_z):
    return [
        [
            ((core * N_SEQ + seq) * N_Y + (y + core) % N_Y) * N_Z + (z + core) % N_Z
            for y in group_y
            for z in group_z
        ]
        for core in range(N_DP)
        for seq in range(N_SEQ)
        for group_y in groups_y
        for group_z in groups_z
    ]


def neighbours(size, start, step):
    place = PLACE_Y if size == N_Y else PLACE_Z
    return [sorted((p, (p + 1) % size), key=lambda q: place[q][step]) for p in range(start, size, 2)]


def forward_kernel(
    core, place_hbm, rows_hbm, cols_hbm, count_hbm, inputs_hbm, out_grad_hbm, ups_hbm, downs_hbm,
    placed_hbm, hidden_t_hbm, pre_grad_t_hbm,
    placed, hidden_t, pre_grad_t, inputs, out_grad, ups, downs, place, rows, cols, count, small_sems, sems, out_sems,
):
    slots, fan = rows.shape
    tok = inputs.shape[0]
    quarter = BLK // 4

    def copies_of(pairs, semaphores):
        return [pltpu.make_async_copy(a, b, semaphores.at[i]) for i, (a, b) in enumerate(pairs)]

    small = copies_of(((rows_hbm, rows), (cols_hbm, cols), (place_hbm, place), (count_hbm, count)), small_sems)
    large = copies_of(
        (
            (inputs_hbm, inputs),
            (ups_hbm.at[0], ups.at[0]),
            (ups_hbm.at[1], ups.at[1]),
            (out_grad_hbm, out_grad),
            (downs_hbm.at[0], downs.at[0]),
            (downs_hbm.at[1], downs.at[1]),
        ),
        sems,
    )
    written = copies_of(
        [(placed.at[:, pl.ds(h * quarter, quarter)], placed_hbm.at[:, pl.ds(h * quarter, quarter)]) for h in range(4)]
        + [(hidden_t, hidden_t_hbm), (pre_grad_t, pre_grad_t_hbm)],
        out_sems,
    )
    for copy in small + large:
        copy.start()
    placed[...] = jnp.zeros_like(placed)
    for copy in small:
        copy.wait()
    slopes = []
    for s in range(slots):
        live = (s < count[0]).astype(jnp.float32)
        for copy in large[:2] if s == 0 else large[2:3]:
            copy.wait()
        pre_act = jnp.zeros((tok, BLK), jnp.float32)
        for k in range(0, fan, 2):
            pre_act += dot_nn(two_blocks(inputs, rows[s, k], rows[s, k + 1]), ups[s, k * BLK : (k + 2) * BLK, :])
        value, slope = gelu_pair(pre_act)
        hidden_t[s] = jnp.transpose(value * live).astype(jnp.bfloat16)
        slopes.append(slope * live)
    written[4].start()
    for s in range(slots):
        for copy in large[3:5] if s == 0 else large[5:]:
            copy.wait()
        hid_grad = jnp.zeros((tok, BLK), jnp.float32)
        for k in range(0, fan, 2):
            hid_grad += dot_nt(
                two_blocks(out_grad, cols[s, k], cols[s, k + 1]),
                jnp.concatenate([downs[s, k * BLK : (k + 1) * BLK, :], downs[s, (k + 1) * BLK : (k + 2) * BLK, :]], axis=1),
            )
        pre_grad_t[s] = jnp.transpose(hid_grad * slopes[s]).astype(jnp.bfloat16)
    written[5].start()
    for h in range(4):
        part = slice(h * quarter, (h + 1) * quarter)
        for s in range(slots):
            turned = pre_grad_t[s]
            for k in range(0, fan, 4):
                edges = [(k + i) * BLK + h * quarter for i in range(4)]
                both = dot_nn(jnp.concatenate([ups[s, e : e + quarter, :] for e in edges], axis=0), turned)
                for i in range(4):
                    at = place[core[0], rows[s, k + i]]
                    product = both[i * quarter : (i + 1) * quarter, :]
                    if s > 0:
                        product += placed[at, part].astype(jnp.float32)
                    placed[at, part] = product.astype(jnp.bfloat16)
        written[h].start()
    for copy in written:
        copy.wait()


def weight_kernel(
    core, seq, rows, cols, inputs, out_grad,
    hidden_t, pre_grad_t, theirs_far, theirs_near, mine_far, mine_near, fetched, sems,
):
    slots = rows.shape[0]
    parts, each = mine_far.shape[0], mine_far.shape[3]
    here, there = core[0] * N_SEQ, (1 - core[0]) * N_SEQ
    flip, mirror, across = seq[0] ^ 1, 3 - seq[0], seq[0] ^ 2
    first = jnp.where(core[0] == 0, flip, mirror)
    second = flip + mirror - first
    targets = (
        (theirs_far, (there + second, there + across)),
        (theirs_near, (there + seq[0], there + first)),
        (mine_far, (here + first, here + across)),
        (mine_near, (here + seq[0], here + second)),
    )
    for half, (data, ids) in enumerate(((inputs, rows), (out_grad, cols))):
        for t, (_, groups) in enumerate(targets):
            for s in range(slots):
                ks = [group * each + i for group in groups for i in range(each)]
                fetch_columns(data, [ids[s, k] for k in ks], fetched.at[half, t, s], sems.at[half, t])
    for half, left in enumerate((pre_grad_t, hidden_t)):
        for t, (target, _) in enumerate(targets):
            wait_for(fetched.at[half, t], sems.at[half, t])
            for s in range(slots):
                for j in range(0, parts * each, 2):
                    pair = jnp.concatenate([fetched[half, t, s, j], fetched[half, t, s, j + 1]], axis=1)
                    both = dot_nn(left[s], pair)
                    for i in range(2):
                        value = both[:, i * BLK : (i + 1) * BLK]
                        target[(j + i) // each, half, s, (j + i) % each] = value.astype(jnp.bfloat16)


def small_call(kernel, out_shape, *operands):
    vmem = pl.BlockSpec(memory_space=pltpu.VMEM)
    return pl.pallas_call(
        kernel,
        out_shape=out_shape,
        in_specs=[vmem] * len(operands),
        out_specs=jax.tree.map(lambda _: vmem, out_shape),
        compiler_params=pltpu.CompilerParams(vmem_limit_bytes=8 * 1024 * 1024),
    )(*operands)


def sum_first_kernel(terms, total):
    value = terms[0].astype(jnp.float32)
    for i in range(1, terms.shape[0]):
        value += terms[i].astype(jnp.float32)
    total[...] = value.astype(jnp.bfloat16)


def sum_first(terms):
    return small_call(sum_first_kernel, jax.ShapeDtypeStruct(terms.shape[1:], terms.dtype), terms)


def sum_large_kernel(terms_hbm, total_hbm, terms, total, sems, out_sems):
    edges = [0, 6, 12, 17, 21, 24]
    pieces = [pl.ds(a, b - a) for a, b in zip(edges, edges[1:])]
    copies = [
        pltpu.make_async_copy(terms_hbm.at[:, piece], terms.at[:, piece], sems.at[i])
        for i, piece in enumerate(pieces)
    ]
    written = [
        pltpu.make_async_copy(total.at[piece], total_hbm.at[piece], out_sems.at[i])
        for i, piece in enumerate(pieces)
    ]
    for copy in copies:
        copy.start()
    for copy, write, piece in zip(copies, written, pieces):
        copy.wait()
        value = terms[0, piece].astype(jnp.float32)
        for i in range(1, terms.shape[0]):
            value += terms[i, piece].astype(jnp.float32)
        total[piece] = value.astype(jnp.bfloat16)
        write.start()
    for write in written:
        write.wait()


def sum_large(terms):
    hbm = pl.BlockSpec(memory_space=pltpu.HBM)
    return pl.pallas_call(
        sum_large_kernel,
        out_shape=jax.ShapeDtypeStruct(terms.shape[1:], terms.dtype),
        in_specs=[hbm],
        out_specs=hbm,
        scratch_shapes=[
            pltpu.VMEM(terms.shape, terms.dtype),
            pltpu.VMEM(terms.shape[1:], terms.dtype),
            pltpu.SemaphoreType.DMA((5,)),
            pltpu.SemaphoreType.DMA((5,)),
        ],
        compiler_params=pltpu.CompilerParams(vmem_limit_bytes=VMEM_LIMIT),
    )(terms)


def add_kernel(*refs):
    *terms, total = refs
    last = total.shape[0]
    value = sum(term[term.shape[0] - last :].astype(jnp.float32) for term in terms)
    total[...] = value.astype(jnp.bfloat16)


def add_last(count, *terms):
    return small_call(add_kernel, jax.ShapeDtypeStruct((count,) + terms[0].shape[1:], terms[0].dtype), *terms)


def weight_end_kernel(*refs):
    *terms, up_grad, down_grad = refs
    slots, each = up_grad.shape[:2]
    for s in range(slots):
        for i in range(each):
            up = sum(term[0, 0, s, i].astype(jnp.float32) for term in terms)
            down = sum(term[0, 1, s, i].astype(jnp.float32) for term in terms)
            up_grad[s, i] = jnp.transpose(up).astype(jnp.bfloat16)
            down_grad[s, i] = down.astype(jnp.bfloat16)


def input_end_kernel(terms, input_grad):
    total = terms[0].astype(jnp.float32)
    for i in range(1, terms.shape[0]):
        total += terms[i].astype(jnp.float32)
    input_grad[...] = jnp.transpose(total).astype(jnp.bfloat16)


def core_seq_pairs(partner):
    return [
        (core * N_SEQ + seq, core * N_SEQ + partner(core, seq)) for core in range(N_DP) for seq in range(N_SEQ)
    ]


def local(inputs, out_grad, up_blocks, down_blocks, up_rows, down_cols, slot_count):
    tok, features = inputs.shape
    slots, fan = up_rows.shape
    each = fan // (N_DP * N_SEQ)
    bf16 = jnp.bfloat16
    smem = pl.BlockSpec(memory_space=pltpu.SMEM)
    vmem = pl.BlockSpec(memory_space=pltpu.VMEM)
    hbm = pl.BlockSpec(memory_space=pltpu.HBM)
    core = lax.axis_index("dp").astype(jnp.int32)
    seq = lax.axis_index("seq").astype(jnp.int32)
    wide = (slots, fan * BLK, BLK)
    placed, hidden_t, pre_grad_t = pl.pallas_call(
        forward_kernel,
        out_shape=(
            jax.ShapeDtypeStruct((N_Y * N_Z, BLK, tok), bf16),
            jax.ShapeDtypeStruct((slots, BLK, tok), bf16),
            jax.ShapeDtypeStruct((slots, BLK, tok), bf16),
        ),
        in_specs=[smem] + [hbm] * 8,
        out_specs=(hbm,) * 3,
        scratch_shapes=[
            pltpu.VMEM((N_Y * N_Z, BLK, tok), bf16),
            pltpu.VMEM((slots, BLK, tok), bf16),
            pltpu.VMEM((slots, BLK, tok), bf16),
            pltpu.VMEM((tok, features), bf16),
            pltpu.VMEM((tok, features), bf16),
            pltpu.VMEM(wide, bf16),
            pltpu.VMEM(wide, bf16),
            pltpu.SMEM((N_DP, N_Y * N_Z), jnp.int32),
            pltpu.SMEM((slots, fan), jnp.int32),
            pltpu.SMEM((slots, fan), jnp.int32),
            pltpu.SMEM((1,), jnp.int32),
            pltpu.SemaphoreType.DMA((4,)),
            pltpu.SemaphoreType.DMA((6,)),
            pltpu.SemaphoreType.DMA((6,)),
        ],
        compiler_params=pltpu.CompilerParams(vmem_limit_bytes=VMEM_LIMIT),
    )(
        core.reshape(1),
        jnp.asarray(place_table(), jnp.int32).reshape(N_DP, N_Y * N_Z),
        up_rows,
        down_cols,
        slot_count,
        inputs,
        out_grad,
        up_blocks.reshape(wide),
        down_blocks.reshape(wide),
    )
    everyone = TOKENS_AX + OWNER_AX
    near = lax.all_to_all(
        placed.reshape(4, 24, BLK, tok), everyone, 0, 0, axis_index_groups=around(owner_groups(neighbours(N_Y, 0, 0), neighbours(N_Z, 0, 0)))
    )

    part_shape = jax.ShapeDtypeStruct((2, 2, slots, each, BLK, BLK), bf16)
    theirs_far, theirs_near, mine_far, mine_near = pl.pallas_call(
        weight_kernel,
        out_shape=(part_shape,) * 4,
        in_specs=[smem] * 4 + [hbm] * 2 + [vmem] * 2,
        out_specs=(vmem,) * 4,
        scratch_shapes=[
            pltpu.VMEM((2, 4, slots, 2 * each, tok, BLK), bf16),
            pltpu.SemaphoreType.DMA((2, 4)),
        ],
        compiler_params=pltpu.CompilerParams(vmem_limit_bytes=12 * 1024 * 1024),
        cost_estimate=pl.CostEstimate(flops=400_000_000, bytes_accessed=10_000_000, transcendentals=0),
    )(core.reshape(1), seq.reshape(1), up_rows, down_cols, inputs, out_grad, hidden_t, pre_grad_t)
    other_core = [(0, 1), (1, 0)]
    far_arrived = lax.ppermute(theirs_far, "dp", other_core)
    near_arrived = lax.ppermute(theirs_near, "dp", other_core)
    first_sent = add_last(2, mine_far, far_arrived)
    first_got = lax.ppermute(first_sent, TOKENS_AX, core_seq_pairs(lambda c, q: 3 - q if c else q ^ 1))
    near, _, _ = lax.optimization_barrier((near, first_sent, near_arrived))
    mid = lax.all_to_all(
        sum_large(near).reshape(4, 6, BLK, tok),
        everyone,
        0,
        0,
        axis_index_groups=around(owner_groups(neighbours(N_Y, 1, 1), neighbours(N_Z, 1, 1))),
    )
    second_got = lax.ppermute(
        add_last(1, mine_near, near_arrived, first_got),
        TOKENS_AX,
        core_seq_pairs(lambda c, q: q ^ 1 if c else 3 - q),
    )
    far = lax.all_to_all(sum_first(mid), everyone, 0, 0, axis_index_groups=owner_groups(FAR_Y, FAR_Z))

    grad_shape = jax.ShapeDtypeStruct((slots, each, BLK, BLK), bf16)
    up_grad, down_grad = small_call(
        weight_end_kernel, (grad_shape, grad_shape), mine_near, near_arrived, first_got, second_got
    )
    input_grad = small_call(input_end_kernel, jax.ShapeDtypeStruct((tok, BLK), bf16), far)
    return input_grad, up_grad, down_grad


def solution(mesh):
    split = Mesh(mesh.devices.reshape(N_DP, N_SEQ, N_Y, N_Z), TOKENS_AX + OWNER_AX)
    in_specs = (
        P(TOKENS_AX, None),
        P(TOKENS_AX, None),
        P(OWNER_AX, None, None, None),
        P(OWNER_AX, None, None, None),
        P(OWNER_AX, None),
        P(OWNER_AX, None),
        P(OWNER_AX),
    )
    out_specs = (
        P(TOKENS_AX, OWNER_AX),
        P(OWNER_AX, TOKENS_AX, None, None),
        P(OWNER_AX, TOKENS_AX, None, None),
    )
    return jax.shard_map(local, mesh=split, in_specs=in_specs, out_specs=out_specs, check_vma=False)
```
